512 devices in a mesh: blk: 64 (over z_hi, y, core), row: 8 (over x, z_lo).
Axes of the slice: x: 4, y: 8, z: 8 (z_hi: 4, z_lo: 2; z = z_hi * 2 + z_lo), core: 2. Of those that a mesh axis runs over, the one named last changes fastest.
Arguments:
- points: float32 [16, 262144], P(None, ('blk', 'row')), may hold values from -6 to 6
- probes: float32 [16, 262144], P(None, ('blk', 'row')), may hold values from -6 to 6
- scales: float32 [16], replicated, may hold values from 0.15 to 0.6
- noise: float32 [1], replicated, may hold values from 0.1 to 1
- pairing: int32 [2], replicated, may hold values from 1 to 63, as said below
Outputs:
- product: float32 [16, 262144], P(None, ('blk', 'row'))
The draws below stay inside these ranges and needn't reach their ends.
Inputs may be any that keep to these rules, and one draw needn't show every extreme that they name: Round r pairs block b with block b XOR pairing[r]; the 2 entries are distinct, and round 0 takes 64 - 1.
All inputs are finite; a program needn't handle non-finite values.
Results may differ from the reference program's by a relative error of at most 0.0003.
Values sent between devices are 32-bit elements; how exact they have to be, the bound alone decides.
No kernel may reach another device: no remote copies, remote signals or barrier semaphores. Data moves between devices by JAX's collectives and lax.ppermute only.
A program may use at most 64 MiB of HBM per device.

```python
import math
import jax
import jax.numpy as jnp
from jax import lax

FEAT = 16
PROBES = 16
ROUNDS = 2
BLOCK = 4096
POINTS = 262144
N_BLK = 64


def draw_pairing(key, part):
    key = jax.random.fold_in(key, 7)
    order = jax.random.permutation(key, N_BLK - 2)
    rest = (order + 1).astype(jnp.int32)
    first = jnp.full((1,), N_BLK - 1, dtype=jnp.int32)
    return jnp.concatenate([first, rest], 0)[:ROUNDS].astype(jnp.int32)


def shard_levels(rng, shape, cuts, low, high):
    def one(dim, blocks):
        steps = jax.random.uniform(jax.random.fold_in(jax.random.fold_in(rng, 6), dim), (blocks,), jnp.float32, low / len(cuts), high / len(cuts))
        return jnp.repeat(jnp.exp(steps), shape[dim] // blocks).reshape((-1,) + (1,) * (len(shape) - dim - 1))

    level = one(*cuts[0])
    for cut in cuts[1:]:
        level = level * one(*cut)
    return level


def scatter_about(rng, extent, deviation, limit, split=(), held_as=jnp.bfloat16):
    array = jax.random.normal(rng, extent, jnp.float32) * deviation
    if len(split) > 0:
        array = shard_levels(rng, extent, split, -0.22, 0.18) * array
    return jnp.clip(array, min=-limit, max=limit).astype(held_as)


def setup_inputs(seed: int = 0) -> dict:
    splits = jax.random.split(jax.random.key(seed), 6)
    points = scatter_about(splits[0], (FEAT, POINTS), 1.0, 6.0, ((1, 512),), jnp.float32)
    probes = scatter_about(splits[1], (PROBES, POINTS), 1.0, 6.0, ((1, 512),), jnp.float32)
    scales = jnp.clip(jnp.exp(jax.random.uniform(splits[2], (FEAT,), jnp.float32, math.log(0.15), math.log(0.6))), 0.15, 0.6)
    noise = jnp.clip(jnp.exp(jax.random.uniform(splits[3], (1,), jnp.float32, math.log(0.1), math.log(1.0))), 0.1, 1.0)
    pairing = draw_pairing(jax.random.fold_in(splits[5], 71), 0)
    return {"points": points, "probes": probes, "scales": scales, "noise": noise, "pairing": pairing}


root_five = 5.0 ** 0.5

def kernel_apply(left, right, right_probes, scales):
    scaled_left = left * scales[:, None]
    scaled_right = right * scales[:, None]
    cross = lax.dot_general(scaled_left, scaled_right, (((0,), (0,)), ((), ())), precision=lax.Precision.HIGHEST, preferred_element_type=jnp.float32)
    squared = lax.optimization_barrier(jnp.sum(scaled_left * scaled_left, 0))[:, None] + lax.optimization_barrier(jnp.sum(scaled_right * scaled_right, 0))[None, :] - 2.0 * cross
    squared = jnp.maximum(squared, 0.0)
    radius = jnp.sqrt(squared)
    tile = (1.0 + root_five * radius + 5.0 / 3.0 * squared) * jnp.exp(-root_five * radius)
    return lax.dot_general(right_probes, tile, (((1,), (1,)), ((), ())), precision=lax.Precision.HIGHEST, preferred_element_type=jnp.float32)

def reference(points, probes, scales, noise, pairing):
    blocks = jnp.transpose(points.reshape(FEAT, N_BLK, BLOCK), (1, 0, 2))
    probe_blocks = jnp.transpose(probes.reshape(PROBES, N_BLK, BLOCK), (1, 0, 2))

    def one_block(index):
        own = blocks[index]
        total = kernel_apply(own, own, probe_blocks[index], scales)
        for step in range(ROUNDS):
            other = jnp.bitwise_xor(index, pairing[step]).astype(jnp.int32)
            total = total + kernel_apply(own, blocks[other], probe_blocks[other], scales)
        return total
    totals = lax.map(one_block, jnp.arange(N_BLK, dtype=jnp.int32))
    summed = jnp.transpose(totals, (1, 0, 2)).reshape(PROBES, POINTS)
    return summed + noise[0] * probes
```

```python
import functools
import math

import jax
import jax.numpy as jnp
from jax import lax
from jax.experimental import pallas as pl
from jax.experimental.pallas import tpu as pltpu
from jax.sharding import PartitionSpec as P

f32 = jnp.float32
bf16 = jnp.bfloat16

log_two = math.log(2.0)
feature_factor = math.sqrt(5.0) / log_two
linear = 3.0 / log_two
constant = 3.0 / log_two**2
probe_factor = log_two**2 / 3.0

tile_y = 512
tile_x = 512


def split_three(value):
    first = value.astype(bf16)
    rest = value - first.astype(f32)
    second = rest.astype(bf16)
    third = (rest - second.astype(f32)).astype(bf16)
    return first, second, third


def norm_rows(scaled, left):
    count = scaled.shape[1]
    norm = jnp.broadcast_to(jnp.sum(scaled * scaled, 0, keepdims=True), (16, count))
    first, second, third = (part.astype(f32) for part in split_three(norm))
    row = lax.broadcasted_iota(jnp.int32, (16, count), 0)
    base = 0 if left else 3
    picked = jnp.where(row == base, first, jnp.where(row == base + 1, second, third))
    inside = (row >= base) & (row < base + 3)
    return jnp.where(inside, picked, jnp.where(row < 6, 1.0, 0.0)).astype(bf16)


def left_rows(scaled):
    a, b, c = split_three(scaled)
    zero = jnp.zeros_like(a)
    return jnp.concatenate([a, a, b, b, a, c, norm_rows(scaled, True), zero], 0)


def right_rows(scaled):
    a, b, c = (-2.0 * part.astype(f32) for part in split_three(scaled))
    a, b, c = a.astype(bf16), b.astype(bf16), c.astype(bf16)
    zero = jnp.zeros_like(a)
    return jnp.concatenate([a, b, a, b, c, a, norm_rows(scaled, False), zero], 0)


def matern(squared):
    squared = jnp.maximum(squared, 1e-30)
    radius = squared * lax.rsqrt(squared)
    return (radius * (radius + linear) + constant) * jnp.exp2(-radius)


def apply_kernel(pieces, has_start, *refs):
    gathered, others, scales = refs[0], refs[1 : 1 + pieces], refs[1 + pieces]
    start = refs[2 + pieces] if has_start else None
    out, left, right, weights = refs[-4:]
    blocks, feat, width = gathered.shape
    scale = scales[...] * feature_factor
    for block in range(blocks):
        left[:, block * width : (block + 1) * width] = left_rows(gathered[block] * scale)
    for index, other in enumerate(others):
        place = slice(index * width, (index + 1) * width)
        right[place, :] = right_rows(other[:feat, :] * scale).T
        probe = other[feat:, :] * probe_factor
        high = probe.astype(bf16)
        low = (probe - high.astype(f32)).astype(bf16)
        weights[:, place] = jnp.concatenate([high, low], 0)
    probes = others[0].shape[0] - feat

    def step(index, _):
        columns = left[:, pl.ds(pl.multiple_of(index * tile_x, tile_x), tile_x)]
        both = jnp.zeros((2 * probes, tile_x), f32)
        fine = jnp.zeros((probes, tile_x), f32)
        for row in range(0, pieces * width, tile_y):
            squared = jnp.dot(right[row : row + tile_y, :], columns, preferred_element_type=f32)
            value = matern(squared)
            high = value.astype(bf16)
            low = (value - high.astype(f32)).astype(bf16)
            weight = weights[:, row : row + tile_y]
            both = both + jnp.dot(weight, high, preferred_element_type=f32)
            fine = fine + jnp.dot(weight[:probes], low, preferred_element_type=f32)
        total = both[:probes] + both[probes:] + fine
        if start is not None:
            total = total + start[index]
        out[index] = total
        return 0

    lax.fori_loop(0, blocks * width // tile_x, step, 0)


def apply_pieces(gathered, others, scales, start=None):
    blocks, feat, width = gathered.shape
    pieces = len(others)
    probes = others[0].shape[0] - feat
    operands = [gathered, *others, scales[:, None]] + ([] if start is None else [start])
    vmem = pl.BlockSpec(memory_space=pltpu.VMEM)
    values = blocks * width * pieces * width
    return pl.pallas_call(
        functools.partial(apply_kernel, pieces, start is not None),
        out_shape=jax.ShapeDtypeStruct((blocks, probes, width), f32),
        in_specs=[vmem] * len(operands),
        out_specs=vmem,
        scratch_shapes=[
            pltpu.VMEM((8 * feat, blocks * width), bf16),
            pltpu.VMEM((pieces * width, 8 * feat), bf16),
            pltpu.VMEM((2 * probes, pieces * width), bf16),
        ],
        compiler_params=pltpu.CompilerParams(vmem_limit_bytes=32 * 2**20),
        cost_estimate=pl.CostEstimate(
            flops=values * 1000, bytes_accessed=values // 8, transcendentals=2 * values
        ),
    )(*operands)


def swap(value, axis, mask):
    pairs = [(source, source ^ mask) for source in range(lax.axis_size(axis))]
    return lax.ppermute(value, axis, pairs)


def body(points, probes, scales, noise, pairing):
    count = lax.axis_size("blk")
    rows = lax.axis_size("row")
    travel = jnp.concatenate([points, probes], 0)

    def branch(mask, points, travel, scales):
        first = swap(travel, "blk", count - 1)
        second = swap(travel, "blk", mask)
        gathered = lax.all_to_all(jnp.broadcast_to(points[None], (rows, *points.shape)), "row", 0, 0)
        part = apply_pieces(gathered, [travel], scales)
        return first, second, gathered, part

    branches = [functools.partial(branch, mask) for mask in range(1, count - 1)]
    first, second, gathered, part = lax.switch(pairing[1] - 1, branches, points, travel, scales)
    part = apply_pieces(gathered, [first, second], scales, part)
    parts = lax.all_to_all(part, "row", 0, 0)
    return jnp.sum(parts, 0) + noise[0] * probes


def solution(mesh):
    in_specs = (P(None, ("blk", "row")), P(None, ("blk", "row")), P(), P(), P())
    out_specs = P(None, ("blk", "row"))
    return jax.shard_map(body, mesh=mesh, in_specs=in_specs, out_specs=out_specs, check_vma=False)
```

```python
import functools
import math

import jax
import jax.numpy as jnp
from jax import lax
from jax.experimental import pallas as pl
from jax.experimental.pallas import tpu as pltpu
from jax.sharding import PartitionSpec as P

f32 = jnp.float32
bf16 = jnp.bfloat16
vmem = pl.BlockSpec(memory_space=pltpu.VMEM)
smem = pl.BlockSpec(memory_space=pltpu.SMEM)
anywhere = pl.BlockSpec(memory_space=pl.ANY)

log_two = math.log(2.0)
feature_factor = math.sqrt(5.0) / log_two
shift = 1.5 / log_two
constant = 0.75 / log_two**2
probe_factor = log_two**2 / 3.0 * 2.0**shift

tile = 256
strip = 32
direct_masks = 34


def split_three(value):
    first = value.astype(bf16)
    rest = value - first.astype(f32)
    second = rest.astype(bf16)
    third = (rest - second.astype(f32)).astype(bf16)
    return first, second, third


def norm_rows(scaled, left):
    count = scaled.shape[1]
    norm = jnp.broadcast_to(jnp.sum(scaled * scaled, 0, keepdims=True), (16, count))
    first, second, third = (part.astype(f32) for part in split_three(norm))
    row = lax.broadcasted_iota(jnp.int32, (16, count), 0)
    base = 0 if left else 3
    picked = jnp.where(row == base, first, jnp.where(row == base + 1, second, third))
    inside = (row >= base) & (row < base + 3)
    return jnp.where(inside, picked, jnp.where(row < 6, 1.0, 0.0)).astype(bf16)


def left_rows(scaled):
    a, b, c = split_three(scaled)
    zero = jnp.zeros_like(a)
    return jnp.concatenate([a, a, b, b, a, c, norm_rows(scaled, True), zero], 0)


def right_rows(scaled):
    a, b, c = (-2.0 * part.astype(f32) for part in split_three(scaled))
    a, b, c = a.astype(bf16), b.astype(bf16), c.astype(bf16)
    zero = jnp.zeros_like(a)
    return jnp.concatenate([a, b, a, b, c, a, norm_rows(scaled, False), zero], 0)


def apply_kernel(pieces, *refs):
    gathered, others, scales, out = refs[0], refs[1 : 1 + pieces], refs[1 + pieces], refs[2 + pieces]
    left, right, weights, distance, coarse, fine = refs[3 + pieces :]
    blocks, feat, width = gathered.shape
    probes = out.shape[1]
    scale = scales[...] * feature_factor
    parts = width // tile

    def prepare(block, _):
        place = pl.ds(pl.multiple_of(block * width, width), width)
        left[:, place] = left_rows(gathered[block] * scale)
        return 0

    lax.fori_loop(0, blocks, prepare, 0)
    for index, other in enumerate(others):
        right[index * width : (index + 1) * width, :] = right_rows(other[:feat, :] * scale).T
        probe = other[feat:, :] * probe_factor
        high = probe.astype(bf16)
        low = (probe - high.astype(f32)).astype(bf16)
        weights[index] = jnp.concatenate([high, low], 0)

    tiles = blocks * parts * pieces

    def place_of(number):
        column = number // pieces
        return column, number - column * pieces

    def find_distance(number, slot):
        column, piece = place_of(jnp.minimum(number, tiles - 1))
        rows = right[pl.ds(pl.multiple_of(piece * width, width), width), :]
        columns = left[:, pl.ds(pl.multiple_of(column * tile, tile), tile)]
        distance[slot] = jnp.dot(rows, columns, preferred_element_type=f32)

    def find_value(slot):
        for row in range(0, width, strip):
            here = slice(row, row + strip)
            squared = jnp.maximum(distance[slot, here, :], 1e-30)
            z = -shift - squared * lax.rsqrt(squared)
            value = (z * z + constant) * jnp.exp2(z)
            high = value.astype(bf16)
            coarse[slot, here, :] = high
            fine[slot, here, :] = (value - high.astype(f32)).astype(bf16)

    def add_product(number, slot):
        column, piece = place_of(jnp.maximum(number, 0))
        weight = weights[piece]
        large = jnp.dot(weight, coarse[slot], preferred_element_type=f32)
        small = jnp.dot(weight[:probes], fine[slot], preferred_element_type=f32)
        total = large[:probes] + large[probes:] + small
        block = column // parts
        place = pl.ds(pl.multiple_of((column - block * parts) * tile, tile), tile)
        before = jnp.where(piece == 0, 0.0, out[block, :, place])
        out[block, :, place] = before + total

    for slot in range(2):
        find_distance(slot, slot)

    def step(index, _):
        for slot in range(2):
            number = 2 * index + slot
            add_product(number - 1, 1 - slot)
            find_value(slot)
            find_distance(number + 2, slot)
        return 0

    lax.fori_loop(0, tiles // 2, step, 0)
    add_product(tiles - 1, 1)


def apply_pieces(gathered, others, scales):
    blocks, feat, width = gathered.shape
    pieces = len(others)
    probes = others[0].shape[0] - feat
    values = blocks * width * pieces * width
    return pl.pallas_call(
        functools.partial(apply_kernel, pieces),
        out_shape=jax.ShapeDtypeStruct((blocks, probes, width), f32),
        in_specs=[vmem] * (2 + pieces),
        out_specs=vmem,
        scratch_shapes=[
            pltpu.VMEM((8 * feat, blocks * width), bf16),
            pltpu.VMEM((pieces * width, 8 * feat), bf16),
            pltpu.VMEM((pieces, 2 * probes, width), bf16),
            pltpu.VMEM((2, width, tile), f32),
            pltpu.VMEM((2, width, tile), bf16),
            pltpu.VMEM((2, width, tile), bf16),
        ],
        compiler_params=pltpu.CompilerParams(vmem_limit_bytes=32 * 2**20),
        cost_estimate=pl.CostEstimate(flops=values * 1000, bytes_accessed=values // 8, transcendentals=2 * values),
        name="apply_pieces",
    )(gathered, *others, scales[:, None])


def pack_kernel(points, probes, pairing, travel, branch, pairing_here, sems):
    feat = points.shape[0]
    third = pltpu.make_async_copy(pairing, pairing_here, sems.at[2])
    third.start()
    first = pltpu.make_async_copy(points, travel.at[:feat], sems.at[0])
    second = pltpu.make_async_copy(probes, travel.at[feat:], sems.at[1])
    first.start()
    second.start()
    third.wait()
    branch[0] = pairing_here[1] - 1
    first.wait()
    second.wait()


def pack(points, probes, pairing):
    rows = points.shape[0] + probes.shape[0]
    return pl.pallas_call(
        pack_kernel,
        out_shape=(
            jax.ShapeDtypeStruct((rows, points.shape[1]), f32),
            jax.ShapeDtypeStruct((1,), jnp.int32),
        ),
        in_specs=[anywhere, anywhere, anywhere],
        out_specs=(vmem, smem),
        scratch_shapes=[pltpu.SMEM((2,), jnp.int32), pltpu.SemaphoreType.DMA((3,))],
        name="pack",
    )(points, probes, pairing)


def spread_kernel(travel, out):
    for block in range(out.shape[0]):
        out[block] = travel[: out.shape[1], :]


def spread(travel, feat, rows):
    return pl.pallas_call(
        spread_kernel,
        out_shape=jax.ShapeDtypeStruct((rows, feat, travel.shape[1]), f32),
        in_specs=[vmem],
        out_specs=vmem,
        cost_estimate=pl.CostEstimate(flops=10**10, bytes_accessed=10**7, transcendentals=0),
        name="spread",
    )(travel)


def swap(value, axis, mask):
    pairs = [(source, source ^ mask) for source in range(lax.axis_size(axis))]
    return lax.ppermute(value, axis, pairs)


def body(points, probes, scales, noise, pairing):
    count = lax.axis_size("blk")
    rows = lax.axis_size("row")
    feat = points.shape[0]
    travel, branch = pack(points, probes, pairing)

    def exchange(mask, travel):
        first = swap(travel, "blk", count - 1)
        direct = mask <= direct_masks
        second = swap(travel, "blk", mask) if direct else swap(first, "blk", mask ^ (count - 1))
        gathered = lax.all_to_all(spread(travel, feat, rows), "row", 0, 0)
        return first, second, gathered

    exchanges = [functools.partial(exchange, mask) for mask in range(1, count - 1)]
    first, second, gathered = lax.switch(branch[0], exchanges, travel)
    part = apply_pieces(gathered, [travel, first, second], scales)
    parts = lax.all_to_all(part, "row", 0, 0)
    return jnp.sum(parts, 0) + noise[0] * probes


def solution(mesh):
    in_specs = (P(None, ("blk", "row")), P(None, ("blk", "row")), P(), P(), P())
    out_specs = P(None, ("blk", "row"))
    return jax.shard_map(body, mesh=mesh, in_specs=in_specs, out_specs=out_specs, check_vma=False)
```

```python
import functools
import math

import jax
import jax.numpy as jnp
from jax import lax
from jax.experimental import pallas as pl
from jax.experimental.pallas import tpu as pltpu
from jax.sharding import PartitionSpec as P

f32 = jnp.float32
bf16 = jnp.bfloat16
vmem = pl.BlockSpec(memory_space=pltpu.VMEM)
smem = pl.BlockSpec(memory_space=pltpu.SMEM)
anywhere = pl.BlockSpec(memory_space=pl.ANY)

log_two = math.log(2.0)
feature_factor = math.sqrt(5.0) / log_two
shift = 1.5 / log_two
constant = 0.75 / log_two**2
probe_factor = log_two**2 / 3.0 * 2.0**shift

tile = 256
strip = 32
direct_masks = 34


def split_three(value):
    first = value.astype(bf16)
    rest = value - first.astype(f32)
    second = rest.astype(bf16)
    third = (rest - second.astype(f32)).astype(bf16)
    return first, second, third


def norm_rows(scaled, left):
    count = scaled.shape[1]
    norm = jnp.broadcast_to(jnp.sum(scaled * scaled, 0, keepdims=True), (16, count))
    first, second, third = (part.astype(f32) for part in split_three(norm))
    row = lax.broadcasted_iota(jnp.int32, (16, count), 0)
    base = 0 if left else 3
    picked = jnp.where(row == base, first, jnp.where(row == base + 1, second, third))
    inside = (row >= base) & (row < base + 3)
    return jnp.where(inside, picked, jnp.where(row < 6, 1.0, 0.0)).astype(bf16)


def left_rows(scaled):
    a, b, c = split_three(scaled)
    zero = jnp.zeros_like(a)
    return jnp.concatenate([a, a, b, b, a, c, norm_rows(scaled, True), zero], 0)


def right_rows(scaled):
    a, b, c = (-2.0 * part.astype(f32) for part in split_three(scaled))
    a, b, c = a.astype(bf16), b.astype(bf16), c.astype(bf16)
    zero = jnp.zeros_like(a)
    return jnp.concatenate([a, b, a, b, c, a, norm_rows(scaled, False), zero], 0)


def apply_kernel(pieces, *refs):
    gathered, others, scales, out = refs[0], refs[1 : 1 + pieces], refs[1 + pieces], refs[2 + pieces]
    left, right, weights, distance, coarse, fine = refs[3 + pieces :]
    blocks, feat, width = gathered.shape
    probes = out.shape[1]
    scale = scales[:, :1]
    parts = width // tile

    def prepare(block, _):
        place = pl.ds(pl.multiple_of(block * width, width), width)
        left[:, place] = left_rows(gathered[block] * scale)
        return 0

    lax.fori_loop(0, blocks, prepare, 0)
    for index, other in enumerate(others):
        right[index * width : (index + 1) * width, :] = right_rows(other[:feat, :] * scale).T
        probe = other[feat:, :] * probe_factor
        high = probe.astype(bf16)
        low = (probe - high.astype(f32)).astype(bf16)
        weights[index] = jnp.concatenate([high, low], 0)

    tiles = blocks * parts * pieces

    def place_of(number):
        column = number // pieces
        return column, number - column * pieces

    def find_distance(number, slot):
        column, piece = place_of(jnp.minimum(number, tiles - 1))
        rows = right[pl.ds(pl.multiple_of(piece * width, width), width), :]
        columns = left[:, pl.ds(pl.multiple_of(column * tile, tile), tile)]
        distance[slot] = jnp.dot(rows, columns, preferred_element_type=f32)

    def find_value(slot):
        for row in range(0, width, strip):
            here = slice(row, row + strip)
            squared = jnp.maximum(distance[slot, here, :], 1e-30)
            z = -shift - squared * lax.rsqrt(squared)
            value = (z * z + constant) * jnp.exp2(z)
            high = value.astype(bf16)
            coarse[slot, here, :] = high
            fine[slot, here, :] = (value - high.astype(f32)).astype(bf16)

    def add_product(number, slot):
        column, piece = place_of(jnp.maximum(number, 0))
        weight = weights[piece]
        large = jnp.dot(weight, coarse[slot], preferred_element_type=f32)
        small = jnp.dot(weight[:probes], fine[slot], preferred_element_type=f32)
        total = large[:probes] + large[probes:] + small
        block = column // parts
        place = pl.ds(pl.multiple_of((column - block * parts) * tile, tile), tile)
        before = jnp.where(piece == 0, 0.0, out[block, :, place])
        out[block, :, place] = before + total

    for slot in range(2):
        find_distance(slot, slot)

    def step(index, _):
        for slot in range(2):
            number = 2 * index + slot
            add_product(number - 1, 1 - slot)
            find_value(slot)
            find_distance(number + 2, slot)
        return 0

    lax.fori_loop(0, tiles // 2, step, 0)
    add_product(tiles - 1, 1)


def apply_pieces(gathered, others, scales):
    blocks, feat, width = gathered.shape
    pieces = len(others)
    probes = others[0].shape[0] - feat
    values = blocks * width * pieces * width
    return pl.pallas_call(
        functools.partial(apply_kernel, pieces),
        out_shape=jax.ShapeDtypeStruct((blocks, probes, width), f32),
        in_specs=[vmem] * (2 + pieces),
        out_specs=vmem,
        scratch_shapes=[
            pltpu.VMEM((8 * feat, blocks * width), bf16),
            pltpu.VMEM((pieces * width, 8 * feat), bf16),
            pltpu.VMEM((pieces, 2 * probes, width), bf16),
            pltpu.VMEM((2, width, tile), f32),
            pltpu.VMEM((2, width, tile), bf16),
            pltpu.VMEM((2, width, tile), bf16),
        ],
        compiler_params=pltpu.CompilerParams(vmem_limit_bytes=10 * 2**20),
        cost_estimate=pl.CostEstimate(flops=values * 1000, bytes_accessed=values // 8, transcendentals=2 * values),
        name="apply_pieces",
    )(gathered, *others, scales)


def pack_kernel(points, probes, scales, pairing, travel, copies, column, branch, once, pairing_here, scales_here, sems):
    feat = points.shape[0]
    third = pltpu.make_async_copy(pairing, pairing_here, sems.at[2])
    third.start()
    fourth = pltpu.make_async_copy(scales, scales_here, sems.at[3])
    fourth.start()
    first = pltpu.make_async_copy(points, travel.at[:feat], sems.at[0])
    second = pltpu.make_async_copy(probes, travel.at[feat:], sems.at[1])
    first.start()
    second.start()
    third.wait()
    branch[0] = pairing_here[1] - 1
    once[0] = jnp.minimum(pairing_here[1], 1)
    fourth.wait()
    row = lax.broadcasted_iota(jnp.int32, column.shape, 0)
    factors = jnp.zeros(column.shape, f32)
    for index in range(feat):
        factors = jnp.where(row == index, scales_here[index] * feature_factor, factors)
    column[...] = factors
    first.wait()
    second.wait()
    for block in range(copies.shape[0]):
        copies[block] = travel[:feat, :]


def pack(points, probes, scales, pairing, rows):
    return pl.pallas_call(
        pack_kernel,
        out_shape=(
            jax.ShapeDtypeStruct((points.shape[0] + probes.shape[0], points.shape[1]), f32),
            jax.ShapeDtypeStruct((rows, *points.shape), f32),
            jax.ShapeDtypeStruct((points.shape[0], 128), f32),
            jax.ShapeDtypeStruct((1,), jnp.int32),
            jax.ShapeDtypeStruct((1,), jnp.int32),
        ),
        in_specs=[anywhere] * 4,
        out_specs=(vmem, vmem, vmem, smem, smem),
        scratch_shapes=[
            pltpu.SMEM((2,), jnp.int32),
            pltpu.SMEM((points.shape[0],), f32),
            pltpu.SemaphoreType.DMA((4,)),
        ],
        name="pack",
    )(points, probes, scales, pairing)


def swap(value, axis, mask):
    pairs = [(source, source ^ mask) for source in range(lax.axis_size(axis))]
    return lax.ppermute(value, axis, pairs)


def body(points, probes, scales, noise, pairing):
    count = lax.axis_size("blk")
    rows = lax.axis_size("row")
    feat = points.shape[0]
    travel, copies, column, branch, once = pack(points, probes, scales, pairing, rows)

    def exchange(mask, travel, once, copies):
        first = swap(travel, "blk", count - 1)
        direct = mask <= direct_masks
        second = swap(travel, "blk", mask) if direct else swap(first, "blk", mask ^ (count - 1))
        gathered = lax.cond(once[0] > 0, lambda copies: lax.all_to_all(copies, "row", 0, 0), lambda copies: copies, copies)
        return first, second, gathered

    exchanges = [functools.partial(exchange, mask) for mask in range(1, count - 1)]
    first, second, gathered = lax.switch(branch[0], exchanges, travel, once, copies)
    part = apply_pieces(gathered, [travel, first, second], column)
    parts = lax.all_to_all(part, "row", 0, 0)
    return jnp.sum(parts, 0) + noise[0] * probes


def solution(mesh):
    in_specs = (P(None, ("blk", "row")), P(None, ("blk", "row")), P(), P(), P())
    out_specs = P(None, ("blk", "row"))
    return jax.shard_map(body, mesh=mesh, in_specs=in_specs, out_specs=out_specs, check_vma=False)
```

```python
import functools
import math

import jax
import jax.numpy as jnp
from jax import lax
from jax.experimental import pallas as pl
from jax.experimental.pallas import tpu as pltpu
from jax.sharding import PartitionSpec as P

f32 = jnp.float32
bf16 = jnp.bfloat16
vmem = pl.BlockSpec(memory_space=pltpu.VMEM)
smem = pl.BlockSpec(memory_space=pltpu.SMEM)
anywhere = pl.BlockSpec(memory_space=pl.ANY)

log_two = math.log(2.0)
feature_factor = math.sqrt(5.0) / log_two
shift = 1.5 / log_two
constant = 0.75 / log_two**2
probe_factor = log_two**2 / 3.0 * 2.0**shift

tile = 256
strip = 32
direct_masks = 34


def split_three(value):
    first = value.astype(bf16)
    rest = value - first.astype(f32)
    second = rest.astype(bf16)
    third = (rest - second.astype(f32)).astype(bf16)
    return first, second, third


def norm_rows(scaled, left):
    count = scaled.shape[1]
    norm = jnp.broadcast_to(jnp.sum(scaled * scaled, 0, keepdims=True), (16, count))
    first, second, third = (part.astype(f32) for part in split_three(norm))
    row = lax.broadcasted_iota(jnp.int32, (16, count), 0)
    base = 0 if left else 3
    picked = jnp.where(row == base, first, jnp.where(row == base + 1, second, third))
    inside = (row >= base) & (row < base + 3)
    return jnp.where(inside, picked, jnp.where(row < 6, 1.0, 0.0)).astype(bf16)


def left_rows(scaled):
    a, b, c = split_three(scaled)
    zero = jnp.zeros_like(a)
    return jnp.concatenate([a, a, b, b, a, c, norm_rows(scaled, True), zero], 0)


def right_rows(scaled):
    a, b, c = (-2.0 * part.astype(f32) for part in split_three(scaled))
    a, b, c = a.astype(bf16), b.astype(bf16), c.astype(bf16)
    zero = jnp.zeros_like(a)
    return jnp.concatenate([a, b, a, b, c, a, norm_rows(scaled, False), zero], 0)


def apply_kernel(pieces, *refs):
    gathered, others, scales, out = refs[0], refs[1 : 1 + pieces], refs[1 + pieces], refs[2 + pieces]
    left, right, weights, distance, coarse, fine = refs[3 + pieces :]
    blocks, feat, width = gathered.shape
    probes = out.shape[1]
    scale = scales[:, :1]
    parts = width // tile

    def prepare(block, _):
        place = pl.ds(pl.multiple_of(block * width, width), width)
        left[:, place] = left_rows(gathered[block] * scale)
        return 0

    lax.fori_loop(0, blocks, prepare, 0, unroll=4)
    for index, other in enumerate(others):
        right[index * width : (index + 1) * width, :] = right_rows(other[:feat, :] * scale).T
        probe = other[feat:, :] * probe_factor
        high = probe.astype(bf16)
        low = (probe - high.astype(f32)).astype(bf16)
        weights[index] = jnp.concatenate([high, low], 0)

    tiles = blocks * parts * pieces

    def place_of(number):
        column = number // pieces
        return column, number - column * pieces

    def find_distance(number, slot):
        column, piece = place_of(jnp.minimum(number, tiles - 1))
        rows = right[pl.ds(pl.multiple_of(piece * width, width), width), :]
        columns = left[:, pl.ds(pl.multiple_of(column * tile, tile), tile)]
        distance[slot] = jnp.dot(rows, columns, preferred_element_type=f32)

    def find_value(slot):
        for row in range(0, width, strip):
            here = slice(row, row + strip)
            squared = jnp.maximum(distance[slot, here, :], 1e-30)
            z = -shift - squared * lax.rsqrt(squared)
            value = (z * z + constant) * jnp.exp2(z)
            high = value.astype(bf16)
            coarse[slot, here, :] = high
            fine[slot, here, :] = (value - high.astype(f32)).astype(bf16)

    def add_product(number, slot):
        column, piece = place_of(jnp.maximum(number, 0))
        weight = weights[piece]
        large = jnp.dot(weight, coarse[slot], preferred_element_type=f32)
        small = jnp.dot(weight[:probes], fine[slot], preferred_element_type=f32)
        total = large[:probes] + large[probes:] + small
        block = column // parts
        place = pl.ds(pl.multiple_of((column - block * parts) * tile, tile), tile)
        before = jnp.where(piece == 0, 0.0, out[block, :, place])
        out[block, :, place] = before + total

    for slot in range(2):
        find_distance(slot, slot)

    def step(index, _):
        for slot in range(2):
            number = 2 * index + slot
            add_product(number - 1, 1 - slot)
            find_value(slot)
            find_distance(number + 2, slot)
        return 0

    lax.fori_loop(0, tiles // 2, step, 0)
    add_product(tiles - 1, 1)


def apply_pieces(gathered, others, scales):
    blocks, feat, width = gathered.shape
    pieces = len(others)
    probes = others[0].shape[0] - feat
    values = blocks * width * pieces * width
    return pl.pallas_call(
        functools.partial(apply_kernel, pieces),
        out_shape=jax.ShapeDtypeStruct((blocks, probes, width), f32),
        in_specs=[vmem] * (2 + pieces),
        out_specs=vmem,
        scratch_shapes=[
            pltpu.VMEM((8 * feat, blocks * width), bf16),
            pltpu.VMEM((pieces * width, 8 * feat), bf16),
            pltpu.VMEM((pieces, 2 * probes, width), bf16),
            pltpu.VMEM((2, width, tile), f32),
            pltpu.VMEM((2, width, tile), bf16),
            pltpu.VMEM((2, width, tile), bf16),
        ],
        compiler_params=pltpu.CompilerParams(vmem_limit_bytes=10 * 2**20),
        cost_estimate=pl.CostEstimate(flops=values * 1000, bytes_accessed=values // 8, transcendentals=2 * values),
        name="apply_pieces",
    )(gathered, *others, scales)


def pack_kernel(points, probes, scales, pairing, travel, copies, column, branch, once, pairing_here, scales_here, sems):
    feat = points.shape[0]
    third = pltpu.make_async_copy(pairing, pairing_here, sems.at[2])
    third.start()
    fourth = pltpu.make_async_copy(scales, scales_here, sems.at[3])
    fourth.start()
    first = pltpu.make_async_copy(points, travel.at[:feat], sems.at[0])
    second = pltpu.make_async_copy(probes, travel.at[feat:], sems.at[1])
    first.start()
    second.start()
    third.wait()
    branch[0] = pairing_here[1] - 1
    once[0] = jnp.minimum(pairing_here[1], 1)
    fourth.wait()
    row = lax.broadcasted_iota(jnp.int32, column.shape, 0)
    factors = jnp.zeros(column.shape, f32)
    for index in range(feat):
        factors = jnp.where(row == index, scales_here[index] * feature_factor, factors)
    column[...] = factors
    first.wait()
    second.wait()
    for block in range(copies.shape[0]):
        copies[block] = travel[:feat, :]


def pack(points, probes, scales, pairing, rows):
    return pl.pallas_call(
        pack_kernel,
        out_shape=(
            jax.ShapeDtypeStruct((points.shape[0] + probes.shape[0], points.shape[1]), f32),
            jax.ShapeDtypeStruct((rows, *points.shape), f32),
            jax.ShapeDtypeStruct((points.shape[0], 128), f32),
            jax.ShapeDtypeStruct((1,), jnp.int32),
            jax.ShapeDtypeStruct((1,), jnp.int32),
        ),
        in_specs=[anywhere] * 4,
        out_specs=(vmem, vmem, vmem, smem, smem),
        scratch_shapes=[
            pltpu.SMEM((2,), jnp.int32),
            pltpu.SMEM((points.shape[0],), f32),
            pltpu.SemaphoreType.DMA((4,)),
        ],
        name="pack",
    )(points, probes, scales, pairing)


def swap(value, axis, mask):
    pairs = [(source, source ^ mask) for source in range(lax.axis_size(axis))]
    return lax.ppermute(value, axis, pairs)


def body(points, probes, scales, noise, pairing):
    count = lax.axis_size("blk")
    rows = lax.axis_size("row")
    feat = points.shape[0]
    travel, copies, column, branch, once = pack(points, probes, scales, pairing, rows)

    def exchange(mask, travel, once, copies):
        first = swap(travel, "blk", count - 1)
        direct = mask <= direct_masks
        second = swap(travel, "blk", mask) if direct else swap(first, "blk", mask ^ (count - 1))
        gathered = lax.cond(once[0] > 0, lambda copies: lax.all_to_all(copies, "row", 0, 0), lambda copies: copies, copies)
        return first, second, gathered

    exchanges = [functools.partial(exchange, mask) for mask in range(1, count - 1)]
    first, second, gathered = lax.switch(branch[0], exchanges, travel, once, copies)
    part = apply_pieces(gathered, [travel, first, second], column)
    parts = lax.all_to_all(part, "row", 0, 0)
    return jnp.sum(parts, 0) + noise[0] * probes


def solution(mesh):
    in_specs = (P(None, ("blk", "row")), P(None, ("blk", "row")), P(), P(), P())
    out_specs = P(None, ("blk", "row"))
    return jax.shard_map(body, mesh=mesh, in_specs=in_specs, out_specs=out_specs, check_vma=False)
```

```python
import functools
import math

import jax
import jax.numpy as jnp
from jax import lax
from jax.experimental import pallas as pl
from jax.experimental.pallas import tpu as pltpu
from jax.sharding import PartitionSpec as P

f32 = jnp.float32
bf16 = jnp.bfloat16
vmem = pl.BlockSpec(memory_space=pltpu.VMEM)
smem = pl.BlockSpec(memory_space=pltpu.SMEM)
anywhere = pl.BlockSpec(memory_space=pl.ANY)

log_two = math.log(2.0)
feature_factor = math.sqrt(5.0) / log_two
shift = 1.5 / log_two
constant = 0.75 / log_two**2
probe_factor = log_two**2 / 3.0 * 2.0**shift

tile = 256
strip = 32
direct_masks = 34


def split_three(value):
    first = value.astype(bf16)
    rest = value - first.astype(f32)
    second = rest.astype(bf16)
    third = (rest - second.astype(f32)).astype(bf16)
    return first, second, third


def norm_rows(scaled, left):
    count = scaled.shape[1]
    norm = jnp.broadcast_to(jnp.sum(scaled * scaled, 0, keepdims=True), (16, count))
    first, second, third = (part.astype(f32) for part in split_three(norm))
    row = lax.broadcasted_iota(jnp.int32, (16, count), 0)
    base = 0 if left else 3
    picked = jnp.where(row == base, first, jnp.where(row == base + 1, second, third))
    inside = (row >= base) & (row < base + 3)
    return jnp.where(inside, picked, jnp.where(row < 6, 1.0, 0.0)).astype(bf16)


def left_rows(scaled):
    a, b, c = split_three(scaled)
    zero = jnp.zeros_like(a)
    return jnp.concatenate([a, a, b, b, a, c, norm_rows(scaled, True), zero], 0)


def right_rows(scaled):
    a, b, c = (-2.0 * part.astype(f32) for part in split_three(scaled))
    a, b, c = a.astype(bf16), b.astype(bf16), c.astype(bf16)
    zero = jnp.zeros_like(a)
    return jnp.concatenate([a, b, a, b, c, a, norm_rows(scaled, False), zero], 0)


def apply_kernel(pieces, *refs):
    gathered, others, scales, out = refs[0], refs[1 : 1 + pieces], refs[1 + pieces], refs[2 + pieces]
    left, right, weights, distance, coarse, fine = refs[3 + pieces :]
    blocks, feat, width = gathered.shape
    probes = out.shape[1]
    scale = scales[...] * feature_factor
    parts = width // tile

    def prepare(block, _):
        place = pl.ds(pl.multiple_of(block * width, width), width)
        left[:, place] = left_rows(gathered[block] * scale)
        return 0

    lax.fori_loop(0, blocks, prepare, 0, unroll=4)
    for index, other in enumerate(others):
        right[index * width : (index + 1) * width, :] = right_rows(other[:feat, :] * scale).T
        probe = other[feat:, :] * probe_factor
        high = probe.astype(bf16)
        low = (probe - high.astype(f32)).astype(bf16)
        weights[index] = jnp.concatenate([high, low], 0)

    tiles = blocks * parts * pieces

    def place_of(number):
        column = number // pieces
        return column, number - column * pieces

    def find_distance(number, slot):
        column, piece = place_of(jnp.minimum(number, tiles - 1))
        rows = right[pl.ds(pl.multiple_of(piece * width, width), width), :]
        columns = left[:, pl.ds(pl.multiple_of(column * tile, tile), tile)]
        distance[slot] = jnp.dot(rows, columns, preferred_element_type=f32)

    def find_value(slot):
        for row in range(0, width, strip):
            here = slice(row, row + strip)
            squared = jnp.maximum(distance[slot, here, :], 1e-30)
            z = -shift - squared * lax.rsqrt(squared)
            value = (z * z + constant) * jnp.exp2(z)
            high = value.astype(bf16)
            coarse[slot, here, :] = high
            fine[slot, here, :] = (value - high.astype(f32)).astype(bf16)

    def add_product(number, slot):
        column, piece = place_of(jnp.maximum(number, 0))
        weight = weights[piece]
        large = jnp.dot(weight, coarse[slot], preferred_element_type=f32)
        small = jnp.dot(weight[:probes], fine[slot], preferred_element_type=f32)
        total = large[:probes] + large[probes:] + small
        block = column // parts
        place = pl.ds(pl.multiple_of((column - block * parts) * tile, tile), tile)
        before = jnp.where(piece == 0, 0.0, out[block, :, place])
        out[block, :, place] = before + total

    for slot in range(2):
        find_distance(slot, slot)

    def step(index, _):
        for slot in range(2):
            number = 2 * index + slot
            add_product(number - 1, 1 - slot)
            find_value(slot)
            find_distance(number + 2, slot)
        return 0

    lax.fori_loop(0, tiles // 2, step, 0)
    add_product(tiles - 1, 1)


def apply_pieces(gathered, others, scales):
    blocks, feat, width = gathered.shape
    pieces = len(others)
    probes = others[0].shape[0] - feat
    values = blocks * width * pieces * width
    return pl.pallas_call(
        functools.partial(apply_kernel, pieces),
        out_shape=jax.ShapeDtypeStruct((blocks, probes, width), f32),
        in_specs=[vmem] * (2 + pieces),
        out_specs=vmem,
        scratch_shapes=[
            pltpu.VMEM((8 * feat, blocks * width), bf16),
            pltpu.VMEM((pieces * width, 8 * feat), bf16),
            pltpu.VMEM((pieces, 2 * probes, width), bf16),
            pltpu.VMEM((2, width, tile), f32),
            pltpu.VMEM((2, width, tile), bf16),
            pltpu.VMEM((2, width, tile), bf16),
        ],
        compiler_params=pltpu.CompilerParams(vmem_limit_bytes=32 * 2**20),
        cost_estimate=pl.CostEstimate(flops=values * 1000, bytes_accessed=values // 8, transcendentals=2 * values),
        name="apply_pieces",
    )(gathered, *others, scales[:, None])


def pack_kernel(points, probes, pairing, travel, branch, pairing_here, sems):
    feat = points.shape[0]
    third = pltpu.make_async_copy(pairing, pairing_here, sems.at[2])
    third.start()
    first = pltpu.make_async_copy(points, travel.at[:feat], sems.at[0])
    second = pltpu.make_async_copy(probes, travel.at[feat:], sems.at[1])
    first.start()
    second.start()
    third.wait()
    branch[0] = pairing_here[1] - 1
    first.wait()
    second.wait()


def pack(points, probes, pairing):
    rows = points.shape[0] + probes.shape[0]
    return pl.pallas_call(
        pack_kernel,
        out_shape=(
            jax.ShapeDtypeStruct((rows, points.shape[1]), f32),
            jax.ShapeDtypeStruct((1,), jnp.int32),
        ),
        in_specs=[anywhere, anywhere, anywhere],
        out_specs=(vmem, smem),
        scratch_shapes=[pltpu.SMEM((2,), jnp.int32), pltpu.SemaphoreType.DMA((3,))],
        name="pack",
    )(points, probes, pairing)


def spread_kernel(travel, out):
    for block in range(out.shape[0]):
        out[block] = travel[: out.shape[1], :]


def spread(travel, feat, rows):
    return pl.pallas_call(
        spread_kernel,
        out_shape=jax.ShapeDtypeStruct((rows, feat, travel.shape[1]), f32),
        in_specs=[vmem],
        out_specs=vmem,
        cost_estimate=pl.CostEstimate(flops=10**10, bytes_accessed=10**7, transcendentals=0),
        name="spread",
    )(travel)


def swap(value, axis, mask):
    pairs = [(source, source ^ mask) for source in range(lax.axis_size(axis))]
    return lax.ppermute(value, axis, pairs)


def body(points, probes, scales, noise, pairing):
    count = lax.axis_size("blk")
    rows = lax.axis_size("row")
    feat = points.shape[0]
    travel, branch = pack(points, probes, pairing)

    def exchange(mask, travel):
        first = swap(travel, "blk", count - 1)
        direct = mask <= direct_masks
        second = swap(travel, "blk", mask) if direct else swap(first, "blk", mask ^ (count - 1))
        gathered = lax.all_to_all(spread(travel, feat, rows), "row", 0, 0)
        return first, second, gathered

    exchanges = [functools.partial(exchange, mask) for mask in range(1, count - 1)]
    first, second, gathered = lax.switch(branch[0], exchanges, travel)
    part = apply_pieces(gathered, [travel, first, second], scales)
    parts = lax.all_to_all(part, "row", 0, 0)
    return jnp.sum(parts, 0) + noise[0] * probes


def solution(mesh):
    in_specs = (P(None, ("blk", "row")), P(None, ("blk", "row")), P(), P(), P())
    out_specs = P(None, ("blk", "row"))
    return jax.shard_map(body, mesh=mesh, in_specs=in_specs, out_specs=out_specs, check_vma=False)
```
